512 devices in a mesh: wide: 64 (over z, x, core), replica: 8 (over y).
Axes of the slice: x: 4, y: 8, z: 8, core: 2. Of those that a mesh axis runs over, the one named last changes fastest.
Arguments:
- node_features: bfloat16 [8, 65536, 128], P('replica', 'wide'), may hold values from -6 to 6
- weight_matrix: bfloat16 [128, 256], replicated, may hold values from -0.5 to 0.5
- bias_term: float32 [256], replicated, may hold values from -3 to 3
- adjacency_tiles: bfloat16 [8, 512, 12, 128, 128], P('replica', 'wide'), may hold values from -0.15625 to 0.15625
- tile_column: int32 [8, 512, 12], P('replica', 'wide'), may hold values from 0 to 511, as said below
- tile_count: int32 [8, 512], P('replica', 'wide'), may hold values from 1 to 12, as said below
- grad_hidden: bfloat16 [8, 65536, 256], P('replica', 'wide'), may hold values from -6 to 6
Outputs:
- hidden_out: bfloat16 [8, 65536, 256], P('replica', 'wide')
- weight_grad: float32 [128, 256], replicated
- bias_grad: float32 [256], replicated
The draws below stay inside these ranges and needn't reach their ends.
Inputs may be any that keep to these rules, and one draw needn't show every extreme that they name: `tile_count`: in every mini-batch some block row has all 12 slots valid. tile_column[b, r, k] differs from r by at most 4, and in every mini-batch both r + 4 and r - 4 occur.
All inputs are finite; a program needn't handle non-finite values.
Results may differ from the reference program's by a relative error of at most 0.012.
Values may be sent and summed in bfloat16 or wider, within the bound.
A program may use at most 128 MiB of HBM per device.

```python
import jax
import jax.numpy as jnp
from jax import lax

IN = 128
HID = 256
TILE = 128
KT = 12
REACH = 4
NB = 512
NODES = 65536
BATCHES = 8


def draw_tile_count(key, part):
    key = jax.random.fold_in(key, 7)
    first, second = jax.random.split(key)
    base = jax.random.randint(first, (BATCHES, NB), 1, KT + 1)
    where_full = jax.random.randint(second, (BATCHES, 1), 0, NB)
    hit = jnp.arange(NB)[None, :] == where_full
    return jnp.where(hit, KT, base).astype(jnp.int32)


def draw_tile_column(key, part):
    key = jax.random.fold_in(key, 11)
    first, second, third = jax.random.split(key, 3)
    row_ids = jnp.arange(NB)[None, :, None]
    slot_zero = jnp.arange(KT)[None, None, :] == 0
    offsets = jax.random.randint(first, (BATCHES, NB, KT), -REACH, REACH + 1)
    up_row = jax.random.randint(second, (BATCHES, 1, 1), REACH, NB // 2)
    down_row = jax.random.randint(third, (BATCHES, 1, 1), NB // 2, NB - REACH)
    offsets = jnp.where(slot_zero & (row_ids == up_row), REACH, offsets)
    offsets = jnp.where(slot_zero & (row_ids == down_row), -REACH, offsets)
    result = jnp.clip(row_ids + offsets, 0, NB - 1)
    result = jnp.where(slot_zero & (row_ids == 0), 0, result)
    result = jnp.where(slot_zero & (row_ids == NB - 1), NB - 1, result)
    return result.astype(jnp.int32)


def steps_of(key, extent, cuts, least, high):
    level, own = 1.0, jax.random.fold_in(key, 6)
    for dim, blocks in cuts:
        draws = jnp.exp(jax.random.uniform(jax.random.fold_in(own, dim), (blocks,), jnp.float32, least / len(cuts), high / len(cuts)))
        level = level * jnp.repeat(draws, extent[dim] // blocks).reshape([-1 if axis == dim else 1 for axis in range(len(extent))])
    return level


def gaussian(key, shape, deviation, bound, cuts=(), kind=jnp.bfloat16):
    loudness = steps_of(key, shape, cuts, -0.22, 0.18) if cuts else 1.0
    array = jax.random.normal(key, shape, jnp.float32) * deviation * loudness
    return jnp.minimum(jnp.maximum(array, -bound), bound).astype(kind)


def setup_inputs(seed: int = 0) -> dict:
    keys = jax.random.split(jax.random.key(seed), 8)
    return {
        "node_features": gaussian(keys[0], (BATCHES, NODES, IN), 1.0, 6.0, ((0, 8), (1, 64))),
        "weight_matrix": gaussian(keys[1], (IN, HID), IN ** -0.5, 0.5),
        "bias_term": gaussian(keys[2], (HID,), 0.5, 3.0, (), jnp.float32),
        "adjacency_tiles": gaussian(keys[3], (BATCHES, NB, KT, TILE, TILE), (KT * TILE) ** -0.5, 0.15625, ((0, 8), (1, 64))),
        "tile_column": draw_tile_column(jax.random.fold_in(keys[7], 71), 0),
        "tile_count": draw_tile_count(jax.random.fold_in(keys[7], 71), 0),
        "grad_hidden": gaussian(keys[6], (BATCHES, NODES, HID), 1.0, 6.0, ((0, 8), (1, 64))),
    }


def one_batch(features, weight_matrix, bias_term, tile_values, columns, counts, grad_out):
    blocks = tile_values.shape[0]
    projected = jnp.dot(features, weight_matrix, preferred_element_type=jnp.float32).astype(jnp.bfloat16)
    slot_mask = (jnp.arange(KT)[None, :] < counts[:, None]).astype(jnp.float32)
    proj_blocks = projected.reshape(blocks, TILE, HID).astype(jnp.float32)

    def forward_row(entry):
        tile_now, col_now, mask_now = entry
        gathered = proj_blocks[col_now] * mask_now[:, None, None]
        return jnp.einsum('kij,kjh->ih', tile_now.astype(jnp.float32), gathered)

    aggregated = lax.map(forward_row, (tile_values, columns, slot_mask)).reshape(-1, HID).astype(jnp.bfloat16)
    preact = aggregated.astype(jnp.float32) + bias_term
    hidden = jax.nn.silu(preact).astype(jnp.bfloat16)
    sigmoid_val = jax.nn.sigmoid(preact)
    grad_pre = (grad_out.astype(jnp.float32) * sigmoid_val * (1.0 + preact * (1.0 - sigmoid_val))).astype(jnp.bfloat16)
    grad_blocks = grad_pre.reshape(blocks, TILE, HID).astype(jnp.float32)

    def backward_row(running, entry):
        tile_now, col_now, mask_now, grad_block = entry
        contrib = jnp.einsum('kij,ih->kjh', tile_now.astype(jnp.float32), grad_block) * mask_now[:, None, None]
        return running.at[col_now].add(contrib), None

    start_total = jnp.zeros((blocks, TILE, HID), jnp.float32)
    grad_proj, _ = lax.scan(backward_row, start_total, (tile_values, columns, slot_mask, grad_blocks))
    grad_proj = grad_proj.reshape(-1, HID)
    grad_weight = jnp.dot(features.astype(jnp.float32).T, grad_proj, precision=lax.Precision.HIGHEST)
    grad_bias = jnp.sum(grad_pre.astype(jnp.float32), axis=0)
    return hidden, grad_weight, grad_bias


def reference(node_features, weight_matrix, bias_term, adjacency_tiles, tile_column, tile_count, grad_hidden):
    outputs = []
    weight_grad = jnp.zeros((IN, HID), jnp.float32)
    bias_grad = jnp.zeros((HID,), jnp.float32)
    for batch in range(BATCHES):
        hidden, grad_weight, grad_bias = one_batch(node_features[batch], weight_matrix, bias_term, adjacency_tiles[batch], tile_column[batch], tile_count[batch], grad_hidden[batch])
        outputs.append(hidden)
        weight_grad = weight_grad + grad_weight
        bias_grad = bias_grad + grad_bias
    return jnp.stack(outputs), weight_grad, bias_grad
```

```python
import functools

import jax
import jax.numpy as jnp
from jax import lax
from jax.experimental import pallas as pl
from jax.experimental.pallas import tpu as pltpu
from jax.sharding import PartitionSpec as P

TILE = 128
KT = 12
REACH = 4
XC = 8
MESH = pl.DeviceIdType.MESH
BF16 = jnp.bfloat16
F32 = jnp.float32


def far_first(n):
    return sorted(range(1, n), key=lambda j: -min(j, n - j))


def kernel(
    sizes,
    x_ref, w_hbm, b_hbm, a_ref, col_hbm, cnt_hbm, gh_ref,
    hid_ref, dw_ref, bg_ref,
    w_ref, b_ref, col_ref, cnt_ref,
    ext, a_buf, gh_buf, hid_buf, ax_buf, acc, bacc,
    s1, r1, s2, r2, s3, r3, s4, r4,
    a_sem, in_sem, halo_send, halo_recv, out_sem, send_sem, recv_sem,
):
    n_xc, n_y, n_z = sizes
    rows = a_buf.shape[0]
    nodes = rows * TILE
    hid = gh_buf.shape[1]
    part = ax_buf.shape[1] // n_xc
    wide = lax.axis_index("wide")
    y = lax.axis_index("replica")
    n_wide = n_xc * n_z
    z = wide // n_xc
    xc = wide % n_xc

    def xc_dev(j):
        return {"wide": z * n_xc + j, "replica": y}

    def y_dev(j):
        return {"wide": wide, "replica": j}

    def z_dev(j):
        return {"wide": j * n_xc + xc, "replica": y}

    after = {"wide": (wide + 1) % n_wide, "replica": y}
    before = {"wide": (wide + n_wide - 1) % n_wide, "replica": y}

    barrier = pltpu.get_barrier_semaphore()
    greeted = 0
    for n, me, dev in ((n_y, y, y_dev), (n_z, z, z_dev), (n_xc, xc, xc_dev)):
        for j in far_first(n):
            pl.semaphore_signal(
                barrier, inc=1, device_id=dev((me + j) % n), device_id_type=MESH
            )
            greeted += 1
    for dev in (after, before):
        pl.semaphore_signal(barrier, inc=1, device_id=dev, device_id_type=MESH)
        greeted += 1

    x_copy = pltpu.make_async_copy(x_ref, ext.at[pl.ds(REACH, rows)], in_sem.at[0])
    x_copy.start()

    def a_copy(r):
        return pltpu.make_async_copy(a_ref.at[0, r], a_buf.at[r], a_sem.at[r])

    for r in range(rows):
        a_copy(r).start()
    gh_copy = pltpu.make_async_copy(gh_ref.at[0], gh_buf, in_sem.at[1])
    gh_copy.start()
    small = [
        pltpu.make_async_copy(src, dst, in_sem.at[2 + i])
        for i, (src, dst) in enumerate(
            ((col_hbm, col_ref), (cnt_hbm, cnt_ref), (w_hbm, w_ref), (b_hbm, b_ref))
        )
    ]
    for copy in small:
        copy.start()

    pl.semaphore_wait(barrier, greeted)

    to_after = pltpu.make_async_remote_copy(
        src_ref=x_ref.at[pl.ds(rows - REACH, REACH)],
        dst_ref=ext.at[pl.ds(0, REACH)],
        send_sem=halo_send.at[0],
        recv_sem=halo_recv.at[0],
        device_id=after,
        device_id_type=MESH,
    )
    to_before = pltpu.make_async_remote_copy(
        src_ref=x_ref.at[pl.ds(0, REACH)],
        dst_ref=ext.at[pl.ds(REACH + rows, REACH)],
        send_sem=halo_send.at[1],
        recv_sem=halo_recv.at[1],
        device_id=before,
        device_id_type=MESH,
    )
    to_after.start()
    to_before.start()
    for copy in small:
        copy.wait()
    x_copy.wait()
    gh_copy.wait()
    to_after.wait()
    to_before.wait()

    first = wide * rows - REACH

    def aggregate(r, carry):
        a_copy(r).wait()
        count = cnt_ref[0, r]
        picked = []
        for k in range(KT):
            block = ext[jnp.clip(col_ref[0, r, k] - first, 0, rows + 2 * REACH - 1)]
            keep = jnp.clip(count - k, 0, 1).astype(F32)
            picked.append(block * jnp.full(block.shape, keep, F32).astype(BF16))
        tiles = jnp.concatenate([a_buf[r, k] for k in range(KT)], axis=1)
        total = jnp.dot(tiles, jnp.concatenate(picked, axis=0), preferred_element_type=F32)
        ax_buf[pl.ds(pl.multiple_of(r * TILE, TILE), TILE), :] = total.astype(BF16)
        return carry

    lax.fori_loop(0, rows, aggregate, 0)

    acc[...] = jnp.zeros_like(acc)
    bacc[...] = jnp.zeros_like(bacc)
    step = 2 * TILE

    def gates(i, carry):
        here = pl.ds(pl.multiple_of(i * step, step), step)
        ax = ax_buf[here, :]
        total = jnp.dot(ax, w_ref[...], preferred_element_type=F32).astype(BF16)
        preact = total.astype(F32) + b_ref[...]
        s = 1.0 / (1.0 + jnp.exp(-preact))
        hid_buf[here, :] = (preact * s).astype(BF16)
        grad = (gh_buf[here, :].astype(F32) * s * (1.0 + preact * (1.0 - s))).astype(BF16)
        acc[...] += lax.dot_general(
            ax, grad, (((0,), (0,)), ((), ())), preferred_element_type=F32
        )
        bacc[...] += jnp.sum(grad.astype(F32).reshape(step // 8, 8, hid), axis=0)
        return carry

    lax.fori_loop(0, nodes // step, gates, 0)

    hid_copy = pltpu.make_async_copy(hid_buf, hid_ref.at[0], out_sem)
    hid_copy.start()

    half = hid // 2
    for j in range(n_xc):
        s1[j, 0:part] = acc[j * part : (j + 1) * part, 0:half].astype(BF16)
        s1[j, part : 2 * part] = acc[j * part : (j + 1) * part, half:hid].astype(BF16)
    bias = jnp.sum(bacc[...], axis=0, keepdims=True)
    row = lax.broadcasted_iota(jnp.int32, (16, half), 0)
    bias = jnp.where(
        row == 0,
        jnp.broadcast_to(bias[:, 0:half], (16, half)),
        jnp.where(row == 1, jnp.broadcast_to(bias[:, half:hid], (16, half)), 0.0),
    ).astype(BF16)
    for j in range(n_xc):
        s1[j, 2 * part : 2 * part + 16] = bias

    def exchange(stage, n, me, dev, src, dst):
        for j in far_first(n):
            to = (me + j) % n
            pltpu.make_async_remote_copy(
                src_ref=src(to),
                dst_ref=dst.at[me],
                send_sem=send_sem.at[stage],
                recv_sem=recv_sem.at[stage],
                device_id=dev(to),
                device_id_type=MESH,
            ).start()

    def arrive(stage, n, dst):
        whole = dst.at[pl.ds(0, n - 1)]
        pltpu.make_async_copy(whole, whole, recv_sem.at[stage]).wait()

    def sent(stage, n, dst):
        whole = dst.at[pl.ds(0, n - 1)]
        pltpu.make_async_copy(whole, whole, send_sem.at[stage]).wait()

    def summed(n, dst):
        total = dst[0].astype(F32)
        for j in range(1, n):
            total += dst[j].astype(F32)
        return total

    exchange(0, n_xc, xc, xc_dev, lambda j: s1.at[j], r1)
    r1[xc] = s1[xc]
    arrive(0, n_xc, r1)
    s2[...] = summed(n_xc, r1).astype(BF16)

    exchange(1, n_y, y, y_dev, lambda j: s2, r2)
    r2[y] = s2[...]
    arrive(1, n_y, r2)
    s3[...] = summed(n_y, r2).astype(BF16)

    exchange(2, n_z, z, z_dev, lambda j: s3, r3)
    r3[z] = s3[...]
    arrive(2, n_z, r3)
    total = summed(n_z, r3)
    s4[...] = total[0 : 2 * part].astype(BF16)

    exchange(3, n_xc, xc, xc_dev, lambda j: s4, r4)
    r4[xc] = s4[...]
    bg_ref[:, 0:half] = total[2 * part : 2 * part + 1]
    bg_ref[:, half:hid] = total[2 * part + 1 : 2 * part + 2]
    arrive(3, n_xc, r4)
    for j in range(n_xc):
        dw_ref[j * part : (j + 1) * part, 0:half] = r4[j, 0:part].astype(F32)
        dw_ref[j * part : (j + 1) * part, half:hid] = r4[j, part : 2 * part].astype(F32)

    hid_copy.wait()
    sent(0, n_xc, r1)
    sent(1, n_y, r2)
    sent(2, n_z, r3)
    sent(3, n_xc, r4)


def on_device(sizes, x, w, b, a, col, cnt, gh):
    n_xc, n_y, n_z = sizes
    _, rows, kt, tile, _ = a.shape
    nodes, width = x.shape[1:]
    hid = w.shape[1]
    part = width // n_xc
    share = (2 * part + 16, hid // 2)
    only = (2 * part, hid // 2)
    hbm = pl.BlockSpec(memory_space=pl.ANY)
    vmem = pl.BlockSpec(memory_space=pltpu.VMEM)
    hidden, dw, bg = pl.pallas_call(
        functools.partial(kernel, sizes),
        out_shape=(
            jax.ShapeDtypeStruct(gh.shape, BF16),
            jax.ShapeDtypeStruct((width, hid), F32),
            jax.ShapeDtypeStruct((1, hid), F32),
        ),
        in_specs=[hbm] * 7,
        out_specs=(hbm, vmem, vmem),
        scratch_shapes=[
            pltpu.VMEM(w.shape, BF16),
            pltpu.VMEM((1, hid), F32),
            pltpu.SMEM(col.shape, jnp.int32),
            pltpu.SMEM(cnt.shape, jnp.int32),
            pltpu.VMEM((rows + 2 * REACH, tile, width), BF16),
            pltpu.VMEM((rows, kt, tile, tile), BF16),
            pltpu.VMEM((nodes, hid), BF16),
            pltpu.VMEM((nodes, hid), BF16),
            pltpu.VMEM((nodes, width), BF16),
            pltpu.VMEM((width, hid), F32),
            pltpu.VMEM((8, hid), F32),
            pltpu.VMEM((n_xc,) + share, BF16),
            pltpu.VMEM((n_xc,) + share, BF16),
            pltpu.VMEM(share, BF16),
            pltpu.VMEM((n_y,) + share, BF16),
            pltpu.VMEM(share, BF16),
            pltpu.VMEM((n_z,) + share, BF16),
            pltpu.VMEM(only, BF16),
            pltpu.VMEM((n_xc,) + only, BF16),
            pltpu.SemaphoreType.DMA((rows,)),
            pltpu.SemaphoreType.DMA((6,)),
            pltpu.SemaphoreType.DMA((2,)),
            pltpu.SemaphoreType.DMA((2,)),
            pltpu.SemaphoreType.DMA,
            pltpu.SemaphoreType.DMA((4,)),
            pltpu.SemaphoreType.DMA((4,)),
        ],
        compiler_params=pltpu.CompilerParams(
            collective_id=0, has_side_effects=True, vmem_limit_bytes=60 * 2**20
        ),
        cost_estimate=pl.CostEstimate(
            flops=2 * rows * kt * tile * tile * width + 4 * nodes * width * hid,
            bytes_accessed=a.size * 2 + x.size * 2 + gh.size * 4,
            transcendentals=nodes * hid,
        ),
        name="graph_layer",
    )(x.reshape(rows, tile, width), w, b.reshape(1, hid), a, col, cnt, gh)
    return hidden, dw, bg.reshape(hid)


def solution(mesh):
    n_wide, n_y = mesh.shape["wide"], mesh.shape["replica"]
    n_xc = min(XC, n_wide // 2)
    return jax.shard_map(
        functools.partial(on_device, (n_xc, n_y, n_wide // n_xc)),
        mesh=mesh,
        in_specs=(
            P("replica", "wide", None),
            P(),
            P(),
            P("replica", "wide", None, None, None),
            P("replica", "wide", None),
            P("replica", "wide"),
            P("replica", "wide", None),
        ),
        out_specs=(P("replica", "wide", None), P(), P()),
        check_vma=False,
    )
```

```python
import functools

import jax
import jax.numpy as jnp
from jax import lax
from jax.experimental import pallas as pl
from jax.experimental.pallas import tpu as pltpu
from jax.sharding import PartitionSpec as P

TILE = 128
KT = 12
REACH = 4
XC = 8
MESH = pl.DeviceIdType.MESH
BF16 = jnp.bfloat16
F32 = jnp.float32


def far_first(n):
    return sorted(range(1, n), key=lambda j: -min(j, n - j))


def kernel(
    sizes,
    x_ref, w_hbm, b_hbm, a_ref, col_hbm, cnt_hbm, gh_ref,
    hid_ref, dw_ref, bg_ref,
    w_ref, b_ref, col_ref, cnt_ref,
    ext, a_buf, gh_buf, ax_buf,
    s1, r1, s2, r2, s3, r3, s4, r4,
    t1, q1, t2, q2, t3, q3,
    a_sem, in_sem, halo_send, halo_recv, send_sem, recv_sem,
):
    n_xc, n_y, n_z = sizes
    rows = a_buf.shape[0]
    nodes = rows * TILE
    hid = gh_buf.shape[1]
    part = ax_buf.shape[1] // n_xc
    wide = lax.axis_index("wide")
    y = lax.axis_index("replica")
    n_wide = n_xc * n_z
    z = wide // n_xc
    xc = wide % n_xc

    def xc_dev(j):
        return {"wide": z * n_xc + j, "replica": y}

    def y_dev(j):
        return {"wide": wide, "replica": j}

    def z_dev(j):
        return {"wide": j * n_xc + xc, "replica": y}

    after = {"wide": (wide + 1) % n_wide, "replica": y}
    before = {"wide": (wide + n_wide - 1) % n_wide, "replica": y}

    barrier = pltpu.get_barrier_semaphore()
    greeted = 0
    for dev in (after, before):
        pl.semaphore_signal(barrier, inc=1, device_id=dev, device_id_type=MESH)
        greeted += 1
    for n, me, dev in ((n_y, y, y_dev), (n_z, z, z_dev), (n_xc, xc, xc_dev)):
        for j in far_first(n):
            pl.semaphore_signal(
                barrier, inc=1, device_id=dev((me + j) % n), device_id_type=MESH
            )
            greeted += 1

    x_copy = pltpu.make_async_copy(x_ref, ext.at[pl.ds(REACH, rows)], in_sem.at[0])
    x_copy.start()

    def a_copy(r):
        return pltpu.make_async_copy(a_ref.at[0, r], a_buf.at[r], a_sem.at[r])

    for r in range(rows):
        a_copy(r).start()
    gh_copy = pltpu.make_async_copy(gh_ref.at[0], gh_buf, in_sem.at[1])
    gh_copy.start()
    small = [
        pltpu.make_async_copy(src, dst, in_sem.at[2 + i])
        for i, (src, dst) in enumerate(
            ((col_hbm, col_ref), (cnt_hbm, cnt_ref), (w_hbm, w_ref), (b_hbm, b_ref))
        )
    ]
    for copy in small:
        copy.start()

    pl.semaphore_wait(barrier, greeted)

    to_after = pltpu.make_async_remote_copy(
        src_ref=x_ref.at[pl.ds(rows - REACH, REACH)],
        dst_ref=ext.at[pl.ds(0, REACH)],
        send_sem=halo_send.at[0],
        recv_sem=halo_recv.at[0],
        device_id=after,
        device_id_type=MESH,
    )
    to_before = pltpu.make_async_remote_copy(
        src_ref=x_ref.at[pl.ds(0, REACH)],
        dst_ref=ext.at[pl.ds(REACH + rows, REACH)],
        send_sem=halo_send.at[1],
        recv_sem=halo_recv.at[1],
        device_id=before,
        device_id_type=MESH,
    )
    to_after.start()
    to_before.start()
    for copy in small:
        copy.wait()
    x_copy.wait()
    gh_copy.wait()
    to_after.wait()
    to_before.wait()

    first = wide * rows - REACH

    for r in range(rows):
        a_copy(r).wait()
        count = cnt_ref[0, r]
        picked = []
        for k in range(KT):
            block = ext[jnp.clip(col_ref[0, r, k] - first, 0, rows + 2 * REACH - 1)]
            keep = jnp.clip(count - k, 0, 1).astype(F32)
            picked.append(block * jnp.full((1, block.shape[1]), keep, F32).astype(BF16))
        tiles = jnp.concatenate([a_buf[r, k] for k in range(KT)], axis=1)
        total = jnp.dot(tiles, jnp.concatenate(picked, axis=0), preferred_element_type=F32)
        ax_buf[r * TILE : (r + 1) * TILE, :] = total.astype(BF16)

    ax = ax_buf[...]
    total = jnp.dot(ax, w_ref[...], preferred_element_type=F32).astype(BF16)
    preact = total.astype(F32) + b_ref[...]
    s = 1.0 / (1.0 + jnp.exp(-preact))
    hid_ref[0] = (preact * s).astype(BF16)
    grad = (gh_buf[...].astype(F32) * s * (1.0 + preact * (1.0 - s))).astype(BF16)
    weight = lax.dot_general(
        ax, grad, (((0,), (0,)), ((), ())), preferred_element_type=F32
    ).astype(BF16)
    bias = jnp.sum(grad.astype(F32).reshape(nodes // 8, 8, hid), axis=0)

    half = hid // 2
    for j in range(n_xc):
        s1[j, 0:part] = weight[j * part : (j + 1) * part, 0:half]
        s1[j, part : 2 * part] = weight[j * part : (j + 1) * part, half:hid]
    t1[...] = jnp.sum(bias, axis=0, keepdims=True)

    def exchange(stage, n, me, dev, src, dst):
        for j in far_first(n):
            to = (me + j) % n
            pltpu.make_async_remote_copy(
                src_ref=src(to),
                dst_ref=dst.at[me],
                send_sem=send_sem.at[stage],
                recv_sem=recv_sem.at[stage],
                device_id=dev(to),
                device_id_type=MESH,
            ).start()

    def arrive(stage, n, dst):
        whole = dst.at[pl.ds(0, n - 1)]
        pltpu.make_async_copy(whole, whole, recv_sem.at[stage]).wait()

    def sent(stage, n, dst):
        whole = dst.at[pl.ds(0, n - 1)]
        pltpu.make_async_copy(whole, whole, send_sem.at[stage]).wait()

    def summed(n, dst):
        total = dst[0].astype(F32)
        for j in range(1, n):
            total += dst[j].astype(F32)
        return total

    exchange(0, n_xc, xc, xc_dev, lambda j: s1.at[j], r1)
    r1[xc] = s1[xc]
    exchange(4, n_xc, xc, xc_dev, lambda j: t1, q1)
    q1[xc] = t1[...]
    arrive(0, n_xc, r1)
    s2[...] = summed(n_xc, r1).astype(BF16)

    exchange(1, n_y, y, y_dev, lambda j: s2, r2)
    r2[y] = s2[...]
    arrive(4, n_xc, q1)
    t2[...] = summed(n_xc, q1)
    exchange(5, n_y, y, y_dev, lambda j: t2, q2)
    q2[y] = t2[...]
    arrive(1, n_y, r2)
    s3[...] = summed(n_y, r2).astype(BF16)

    exchange(2, n_z, z, z_dev, lambda j: s3, r3)
    r3[z] = s3[...]
    arrive(5, n_y, q2)
    t3[...] = summed(n_y, q2)
    exchange(6, n_z, z, z_dev, lambda j: t3, q3)
    q3[z] = t3[...]
    arrive(2, n_z, r3)
    s4[...] = summed(n_z, r3).astype(BF16)

    exchange(3, n_xc, xc, xc_dev, lambda j: s4, r4)
    r4[xc] = s4[...]
    arrive(6, n_z, q3)
    bg_ref[...] = summed(n_z, q3)
    sent(0, n_xc, r1)
    sent(1, n_y, r2)
    sent(2, n_z, r3)
    sent(4, n_xc, q1)
    sent(5, n_y, q2)
    sent(6, n_z, q3)
    arrive(3, n_xc, r4)
    for j in range(n_xc):
        dw_ref[j * part : (j + 1) * part, 0:half] = r4[j, 0:part].astype(F32)
        dw_ref[j * part : (j + 1) * part, half:hid] = r4[j, part : 2 * part].astype(F32)
    sent(3, n_xc, r4)


def finish(h_in, w_in, b_in, h_out, w_out, b_out, sem):
    pairs = ((h_in, h_out), (w_in, w_out), (b_in, b_out))
    copies = [pltpu.make_async_copy(a, b, sem.at[i]) for i, (a, b) in enumerate(pairs)]
    for copy in copies:
        copy.start()
    for copy in copies:
        copy.wait()


def on_device(sizes, x, w, b, a, col, cnt, gh):
    n_xc, n_y, n_z = sizes
    _, rows, kt, tile, _ = a.shape
    nodes, width = x.shape[1:]
    hid = w.shape[1]
    part = width // n_xc
    share = (2 * part, hid // 2)
    flat = (1, hid)
    hbm = pl.BlockSpec(memory_space=pltpu.HBM)
    free = pl.BlockSpec(memory_space=pl.ANY)
    vmem = pl.BlockSpec(memory_space=pltpu.VMEM)
    operands = (x.reshape(rows, tile, width), w, b.reshape(1, hid), a, col, cnt, gh)
    hidden, dw, bg = pl.pallas_call(
        functools.partial(kernel, sizes),
        out_shape=(
            pltpu.VMEM(gh.shape, BF16),
            pltpu.VMEM((width, hid), F32),
            pltpu.VMEM((1, hid), F32),
        ),
        in_specs=[hbm] * 7,
        out_specs=(vmem,) * 3,
        scratch_shapes=[
            pltpu.VMEM(w.shape, BF16),
            pltpu.VMEM((1, hid), F32),
            pltpu.SMEM(col.shape, jnp.int32),
            pltpu.SMEM(cnt.shape, jnp.int32),
            pltpu.VMEM((rows + 2 * REACH, tile, width), BF16),
            pltpu.VMEM((rows, kt, tile, tile), BF16),
            pltpu.VMEM((nodes, hid), BF16),
            pltpu.VMEM((nodes, width), BF16),
            pltpu.VMEM((n_xc,) + share, BF16),
            pltpu.VMEM((n_xc,) + share, BF16),
            pltpu.VMEM(share, BF16),
            pltpu.VMEM((n_y,) + share, BF16),
            pltpu.VMEM(share, BF16),
            pltpu.VMEM((n_z,) + share, BF16),
            pltpu.VMEM(share, BF16),
            pltpu.VMEM((n_xc,) + share, BF16),
            pltpu.VMEM(flat, F32),
            pltpu.VMEM((n_xc,) + flat, F32),
            pltpu.VMEM(flat, F32),
            pltpu.VMEM((n_y,) + flat, F32),
            pltpu.VMEM(flat, F32),
            pltpu.VMEM((n_z,) + flat, F32),
            pltpu.SemaphoreType.DMA((rows,)),
            pltpu.SemaphoreType.DMA((6,)),
            pltpu.SemaphoreType.DMA((2,)),
            pltpu.SemaphoreType.DMA((2,)),
            pltpu.SemaphoreType.DMA((7,)),
            pltpu.SemaphoreType.DMA((7,)),
        ],
        compiler_params=pltpu.CompilerParams(
            collective_id=0, has_side_effects=True, vmem_limit_bytes=40 * 2**20
        ),
        cost_estimate=pl.CostEstimate(
            flops=2 * rows * kt * tile * tile * width + 4 * nodes * width * hid,
            bytes_accessed=a.size * 2 + x.size * 2 + gh.size * 4,
            transcendentals=nodes * hid,
        ),
        name="graph_layer",
    )(*(pltpu.with_memory_space_constraint(t, pltpu.HBM) for t in operands))
    hidden, dw, bg = pl.pallas_call(
        finish,
        out_shape=tuple(jax.ShapeDtypeStruct(v.shape, v.dtype) for v in (hidden, dw, bg)),
        in_specs=[free] * 3,
        out_specs=(hbm,) * 3,
        scratch_shapes=[pltpu.SemaphoreType.DMA((3,))],
        compiler_params=pltpu.CompilerParams(vmem_limit_bytes=40 * 2**20),
        name="finish",
    )(hidden, dw, bg)
    return hidden, dw, bg.reshape(hid)


def solution(mesh):
    n_wide, n_y = mesh.shape["wide"], mesh.shape["replica"]
    n_xc = min(XC, n_wide // 2)
    return jax.shard_map(
        functools.partial(on_device, (n_xc, n_y, n_wide // n_xc)),
        mesh=mesh,
        in_specs=(
            P("replica", "wide", None),
            P(),
            P(),
            P("replica", "wide", None, None, None),
            P("replica", "wide", None),
            P("replica", "wide"),
            P("replica", "wide", None),
        ),
        out_specs=(P("replica", "wide", None), P(), P()),
        check_vma=False,
    )
```

```python
import functools

import jax
import jax.numpy as jnp
from jax import lax
from jax.experimental import pallas as pl
from jax.experimental.pallas import tpu as pltpu
from jax.sharding import PartitionSpec as P

TILE = 128
KT = 12
REACH = 4
XC = 8
MESH = pl.DeviceIdType.MESH
BF16 = jnp.bfloat16
F32 = jnp.float32


def far_first(n):
    return sorted(range(1, n), key=lambda j: -min(j, n - j))


def at_distance(n, d):
    return sorted({d % n, (n - d) % n} - {0})


def kernel(
    sizes,
    x_hbm, w_hbm, b_hbm, a_hbm, col_hbm, cnt_hbm, gh_hbm,
    hid_ref, dw_ref, bg_ref,
    w_ref, b_ref, col_ref, cnt_ref,
    x_ref, halo, a_ref, gh_ref, near, grouped, bacc, acc,
    s1, r1, s2, r2, s3, r3, s4, r4,
    t1, q1, t2, q2, t3, q3,
    a_sem, in_sem, halo_send, halo_recv, send_sem, recv_sem, relay,
):
    n_xc, n_y, n_z = sizes
    rows = a_ref.shape[0]
    nodes = rows * TILE
    hid = gh_ref.shape[1]
    width = x_ref.shape[2]
    part = width // n_xc
    wide = lax.axis_index("wide")
    y = lax.axis_index("replica")
    n_wide = n_xc * n_z
    z = wide // n_xc
    xc = wide % n_xc

    def xc_dev(j):
        return {"wide": z * n_xc + j, "replica": y}

    def y_dev(j):
        return {"wide": wide, "replica": j}

    def z_dev(j):
        return {"wide": j * n_xc + xc, "replica": y}

    after = {"wide": (wide + 1) % n_wide, "replica": y}
    before = {"wide": (wide + n_wide - 1) % n_wide, "replica": y}

    barrier = pltpu.get_barrier_semaphore()

    def greet(dev):
        pl.semaphore_signal(barrier, inc=1, device_id=dev, device_id_type=MESH)

    rings = ((n_y, y, y_dev), (n_z, z, z_dev))
    greet(after)
    greet(before)
    x_copy = pltpu.make_async_copy(x_hbm, x_ref, in_sem.at[0])
    x_copy.start()
    greeted = 2
    for n, me, dev in rings:
        for j in at_distance(n, 1):
            greet(dev((me + j) % n))
            greeted += 1
    for j in far_first(n_xc):
        greet(xc_dev((xc + j) % n_xc))
        greeted += 1

    small = [
        pltpu.make_async_copy(src, dst, in_sem.at[2 + i])
        for i, (src, dst) in enumerate(
            ((col_hbm, col_ref), (cnt_hbm, cnt_ref), (w_hbm, w_ref), (b_hbm, b_ref))
        )
    ]
    for copy in small:
        copy.start()

    def a_copy(r):
        return pltpu.make_async_copy(a_hbm.at[0, r], a_ref.at[r], a_sem.at[r])

    for r in range(rows):
        a_copy(r).start()
    gh_copy = pltpu.make_async_copy(gh_hbm.at[0], gh_ref, in_sem.at[1])
    gh_copy.start()

    x_copy.wait()
    pl.semaphore_wait(barrier, greeted)

    def halo_copy(side):
        start = rows - REACH if side == 0 else 0
        return pltpu.make_async_remote_copy(
            src_ref=x_ref.at[pl.ds(start, REACH)],
            dst_ref=halo.at[side],
            send_sem=halo_send.at[side],
            recv_sem=halo_recv.at[side],
            device_id=after if side == 0 else before,
            device_id_type=MESH,
        )

    halo_copy(0).start()
    halo_copy(1).start()

    def vouch(ring, d):
        n, me, dev = rings[ring]
        for j in at_distance(n, d):
            pl.semaphore_signal(
                relay.at[ring, d - 1], inc=1, device_id=dev((me + j) % n), device_id_type=MESH
            )

    def heard(ring, d):
        count = len(at_distance(rings[ring][0], d))
        if count:
            pl.semaphore_wait(relay.at[ring, d - 1], count)

    vouch(0, 1)
    vouch(1, 1)
    for copy in small:
        copy.wait()
    heard(0, 1)
    heard(1, 1)
    vouch(0, 2)
    vouch(1, 2)

    first = wide * rows
    for r in range(rows):
        a_copy(r).wait()
        count = cnt_ref[0, r]
        picked = []
        for k in range(KT):
            col = col_ref[0, r, k] - first
            inside = jnp.clip(col, 0, rows - 1)
            own = 1 - jnp.minimum(jnp.abs(col - inside), 1)
            keep = (jnp.clip(count - k, 0, 1) * own).astype(F32)
            block = x_ref[inside]
            picked.append(block * jnp.full((1, width), keep, F32).astype(BF16))
        tiles = jnp.concatenate([a_ref[r, k] for k in range(KT)], axis=1)
        near[r] = jnp.dot(tiles, jnp.concatenate(picked, axis=0), preferred_element_type=F32)

    piece = TILE // 4
    for r in range(rows):
        count = cnt_ref[0, r]
        low = r < REACH
        blocks = range(r, REACH) if low else range(0, r - rows + REACH + 1)
        base = first - REACH if low else first + rows
        weights = {}
        for h in blocks:
            for k in range(KT):
                off = jnp.minimum(jnp.abs(col_ref[0, r, k] - base - h), 1)
                weights[h, k] = (jnp.clip(count - k, 0, 1) * (1 - off)).astype(F32)
        for q in range(TILE // piece):
            here = slice(q * piece, (q + 1) * piece)
            sums = {h: None for h in blocks}
            for k in range(KT):
                tile = a_ref[r, k, here, :].astype(F32)
                for h in blocks:
                    term = tile * weights[h, k]
                    sums[h] = term if sums[h] is None else sums[h] + term
            for h in range(REACH):
                lanes = slice(h * TILE, (h + 1) * TILE)
                if h in blocks:
                    grouped[r, here, lanes] = sums[h].astype(BF16)
                else:
                    grouped[r, here, lanes] = jnp.zeros((piece, TILE), BF16)

    gh_copy.wait()
    some = REACH * TILE

    def half_pass(side):
        base = side * REACH
        pltpu.make_async_copy(halo.at[side], halo.at[side], halo_recv.at[side]).wait()
        blocks = jnp.concatenate([halo[side, h] for h in range(REACH)], axis=0)
        ax = jnp.concatenate(
            [
                near[base + i] + jnp.dot(grouped[base + i], blocks, preferred_element_type=F32)
                for i in range(REACH)
            ],
            axis=0,
        ).astype(BF16)
        here = pl.ds(pl.multiple_of(side * some, some), some)
        total = jnp.dot(ax, w_ref[...], preferred_element_type=F32).astype(BF16)
        preact = total.astype(F32) + b_ref[...]
        s = 1.0 / (1.0 + jnp.exp(-preact))
        hid_ref[0, here, :] = (preact * s).astype(BF16)
        grad = (gh_ref[here, :].astype(F32) * s * (1.0 + preact * (1.0 - s))).astype(BF16)
        weight = lax.dot_general(
            ax, grad, (((0,), (0,)), ((), ())), preferred_element_type=F32
        )
        return weight, jnp.sum(grad.astype(F32).reshape(some // 8, 8, hid), axis=0)

    sooner = 1 - wide % 2
    weight, bias = half_pass(sooner)
    acc[...] = weight
    bacc[...] = bias
    weight, bias = half_pass(1 - sooner)
    weight = (acc[...] + weight).astype(BF16)
    bias = bacc[...] + bias

    half = hid // 2
    for j in range(n_xc):
        s1[j, 0:part] = weight[j * part : (j + 1) * part, 0:half]
        s1[j, part : 2 * part] = weight[j * part : (j + 1) * part, half:hid]
    t1[...] = jnp.sum(bias, axis=0, keepdims=True)

    def exchange(stage, n, me, dev, src, dst):
        for j in far_first(n):
            to = (me + j) % n
            pltpu.make_async_remote_copy(
                src_ref=src(to),
                dst_ref=dst.at[me],
                send_sem=send_sem.at[stage],
                recv_sem=recv_sem.at[stage],
                device_id=dev(to),
                device_id_type=MESH,
            ).start()

    def arrive(stage, n, dst):
        whole = dst.at[pl.ds(0, n - 1)]
        pltpu.make_async_copy(whole, whole, recv_sem.at[stage]).wait()

    def sent(stage, n, dst):
        whole = dst.at[pl.ds(0, n - 1)]
        pltpu.make_async_copy(whole, whole, send_sem.at[stage]).wait()

    def summed(n, dst):
        total = dst[0].astype(F32)
        for j in range(1, n):
            total += dst[j].astype(F32)
        return total

    exchange(0, n_xc, xc, xc_dev, lambda j: s1.at[j], r1)
    r1[xc] = s1[xc]
    exchange(4, n_xc, xc, xc_dev, lambda j: t1, q1)
    q1[xc] = t1[...]
    arrive(0, n_xc, r1)
    s2[...] = summed(n_xc, r1).astype(BF16)
    heard(0, 2)
    heard(1, 2)

    exchange(1, n_y, y, y_dev, lambda j: s2, r2)
    r2[y] = s2[...]
    arrive(4, n_xc, q1)
    t2[...] = summed(n_xc, q1)
    exchange(5, n_y, y, y_dev, lambda j: t2, q2)
    q2[y] = t2[...]
    arrive(1, n_y, r2)
    s3[...] = summed(n_y, r2).astype(BF16)

    exchange(2, n_z, z, z_dev, lambda j: s3, r3)
    r3[z] = s3[...]
    arrive(5, n_y, q2)
    t3[...] = summed(n_y, q2)
    exchange(6, n_z, z, z_dev, lambda j: t3, q3)
    q3[z] = t3[...]
    arrive(2, n_z, r3)
    s4[...] = summed(n_z, r3).astype(BF16)

    exchange(3, n_xc, xc, xc_dev, lambda j: s4, r4)
    r4[xc] = s4[...]
    arrive(6, n_z, q3)
    bg_ref[...] = summed(n_z, q3)
    halo_copy(0).wait_send()
    halo_copy(1).wait_send()
    sent(0, n_xc, r1)
    sent(1, n_y, r2)
    sent(2, n_z, r3)
    sent(4, n_xc, q1)
    sent(5, n_y, q2)
    sent(6, n_z, q3)
    arrive(3, n_xc, r4)
    for j in range(n_xc):
        dw_ref[j * part : (j + 1) * part, 0:half] = r4[j, 0:part].astype(F32)
        dw_ref[j * part : (j + 1) * part, half:hid] = r4[j, part : 2 * part].astype(F32)
    sent(3, n_xc, r4)


def finish(h_in, w_in, b_in, h_out, w_out, b_out, sem):
    pairs = ((h_in, h_out), (w_in, w_out), (b_in, b_out))
    copies = [pltpu.make_async_copy(a, b, sem.at[i]) for i, (a, b) in enumerate(pairs)]
    for copy in copies:
        copy.start()
    for copy in copies:
        copy.wait()


def on_device(sizes, x, w, b, a, col, cnt, gh):
    n_xc, n_y, n_z = sizes
    _, rows, kt, tile, _ = a.shape
    nodes, width = x.shape[1:]
    hid = w.shape[1]
    part = width // n_xc
    share = (2 * part, hid // 2)
    flat = (1, hid)
    hbm = pl.BlockSpec(memory_space=pltpu.HBM)
    free = pl.BlockSpec(memory_space=pl.ANY)
    vmem = pl.BlockSpec(memory_space=pltpu.VMEM)
    operands = (x.reshape(rows, tile, width), w, b.reshape(1, hid), a, col, cnt, gh)
    hidden, dw, bg = pl.pallas_call(
        functools.partial(kernel, sizes),
        out_shape=(
            pltpu.VMEM(gh.shape, BF16),
            pltpu.VMEM((width, hid), F32),
            pltpu.VMEM((1, hid), F32),
        ),
        in_specs=[hbm] * 7,
        out_specs=(vmem,) * 3,
        scratch_shapes=[
            pltpu.VMEM(w.shape, BF16),
            pltpu.VMEM((1, hid), F32),
            pltpu.SMEM(col.shape, jnp.int32),
            pltpu.SMEM(cnt.shape, jnp.int32),
            pltpu.VMEM((rows, tile, width), BF16),
            pltpu.VMEM((2, REACH, tile, width), BF16),
            pltpu.VMEM((rows, kt, tile, tile), BF16),
            pltpu.VMEM((nodes, hid), BF16),
            pltpu.VMEM((rows, tile, width), F32),
            pltpu.VMEM((rows, tile, REACH * tile), BF16),
            pltpu.VMEM((8, hid), F32),
            pltpu.VMEM((width, hid), F32),
            pltpu.VMEM((n_xc,) + share, BF16),
            pltpu.VMEM((n_xc,) + share, BF16),
            pltpu.VMEM(share, BF16),
            pltpu.VMEM((n_y,) + share, BF16),
            pltpu.VMEM(share, BF16),
            pltpu.VMEM((n_z,) + share, BF16),
            pltpu.VMEM(share, BF16),
            pltpu.VMEM((n_xc,) + share, BF16),
            pltpu.VMEM(flat, F32),
            pltpu.VMEM((n_xc,) + flat, F32),
            pltpu.VMEM(flat, F32),
            pltpu.VMEM((n_y,) + flat, F32),
            pltpu.VMEM(flat, F32),
            pltpu.VMEM((n_z,) + flat, F32),
            pltpu.SemaphoreType.DMA((rows,)),
            pltpu.SemaphoreType.DMA((6,)),
            pltpu.SemaphoreType.DMA((2,)),
            pltpu.SemaphoreType.DMA((2,)),
            pltpu.SemaphoreType.DMA((7,)),
            pltpu.SemaphoreType.DMA((7,)),
            pltpu.SemaphoreType.REGULAR((2, 2)),
        ],
        compiler_params=pltpu.CompilerParams(
            collective_id=0, has_side_effects=True, vmem_limit_bytes=40 * 2**20
        ),
        cost_estimate=pl.CostEstimate(
            flops=2 * rows * kt * tile * tile * width + 4 * nodes * width * hid,
            bytes_accessed=a.size * 2 + x.size * 2 + gh.size * 4,
            transcendentals=nodes * hid,
        ),
        name="graph_layer",
    )(*(pltpu.with_memory_space_constraint(t, pltpu.HBM) for t in operands))
    hidden, dw, bg = pl.pallas_call(
        finish,
        out_shape=tuple(jax.ShapeDtypeStruct(v.shape, v.dtype) for v in (hidden, dw, bg)),
        in_specs=[free] * 3,
        out_specs=(hbm,) * 3,
        scratch_shapes=[pltpu.SemaphoreType.DMA((3,))],
        compiler_params=pltpu.CompilerParams(vmem_limit_bytes=40 * 2**20),
        name="finish",
    )(hidden, dw, bg)
    return hidden, dw, bg.reshape(hid)


def solution(mesh):
    n_wide, n_y = mesh.shape["wide"], mesh.shape["replica"]
    n_xc = min(XC, n_wide // 2)
    return jax.shard_map(
        functools.partial(on_device, (n_xc, n_y, n_wide // n_xc)),
        mesh=mesh,
        in_specs=(
            P("replica", "wide", None),
            P(),
            P(),
            P("replica", "wide", None, None, None),
            P("replica", "wide", None),
            P("replica", "wide"),
            P("replica", "wide", None),
        ),
        out_specs=(P("replica", "wide", None), P(), P()),
        check_vma=False,
    )
```
